32 devices in a mesh: groups: 2 (over y), cluster: 4 (over z), helper: 2 (over x), rep: 2 (over core).
Axes of the slice: x: 2, y: 2, z: 4, core: 2. Of those that a mesh axis runs over, the one named last changes fastest.
Arguments:
- embeddings: bfloat16 [8192, 1024], P(('groups', 'cluster', 'helper', 'rep')), parts along dimension 0, may hold values from -6 to 6
- labels: int32 [8192, 1], P(('groups', 'cluster', 'helper', 'rep')), parts along dimension 0, may hold values from 0 to 3; in each aligned block of 256 rows (0 to 255, 256 to 511, ...) at most 128 rows name the same one
- priority: int32 [8192], P(('groups', 'cluster', 'helper', 'rep')), parts along dimension 0, may hold values from 0 to 4095
Outputs:
- best_cosine: float32 [8192], P(('groups', 'cluster', 'helper', 'rep')), parts along dimension 0
The draws below stay inside these ranges and needn't reach their ends.
There are 2 independent parts, one for each index of `groups`. The reference program is written for one: setup_inputs(seed, part) draws one part's arguments, and reference() takes and returns one part's arrays. A program takes and returns all parts, laid end to end along the dimension named above; each array names one. Nothing has to cross between parts.
Inputs may be any that keep to these rules, and one draw needn't show every extreme that they name: `labels`: in the rows of one device no cluster is named more than 128 times, and in some devices' rows some cluster exactly 128 times; every cluster is named.
All inputs are finite; a program needn't handle non-finite values.
Results may differ from the reference program's by a relative error of at most 0.0014.
Values may be sent and summed in bfloat16 or wider, within the bound.
No kernel may reach another device: no remote copies, remote signals or barrier semaphores. Data moves between devices by JAX's collectives and lax.ppermute only.
A program may use at most 64 MiB of HBM per device.

```python
import math
import jax
import jax.numpy as jnp
import numpy as np
from jax import lax

D = 1024
ROW_DEV = 256
CLUSTERS = 4
CAP = 128
ROWS = 4096


def with_ends(result, stream_key, low, top_value):
    extent = result.shape
    spot = [jax.random.randint(jax.random.fold_in(stream_key, axis), (), 0, extent[axis]) for axis in range(len(extent))]
    result = result.at[tuple(spot)].set(low)
    longest = extent.index(max(extent))
    spot[longest] = (spot[longest] + 1) % extent[longest]
    return result.at[tuple(spot)].set(top_value)


def level_of(key, dims, split, low, high):
    factor_of = 1.0
    for dim, blocks in split:
        draws = jax.random.uniform(jax.random.fold_in(jax.random.fold_in(key, 6), dim), (blocks,), jnp.float32, low / len(split), high / len(split))
        factor_of = factor_of * jnp.repeat(jnp.exp(draws), dims[dim] // blocks).reshape((-1,) + (1,) * (len(dims) - 1 - dim))
    return factor_of


def shared_out(stream_key, own, number, rows, amount, top, bound, slope):
    sequence = jax.random.permutation(stream_key, amount)
    heavy_load, ordinary = load_shares(amount, rows * top, bound, slope, True), load_shares(amount, rows * top, bound, slope, False)
    places = jnp.arange(amount)

    def named(lengths, turn):
        used = int((lengths > 0).sum())
        fixed = max(1, used // 4)
        moved = fixed + (places - fixed + turn * (used - fixed)) % max(1, amount - fixed)
        return jnp.zeros((amount,), jnp.int32).at[sequence[jnp.where(places < fixed, places, moved)]].set(jnp.asarray(lengths, jnp.int32))

    lengths = jnp.where(number % 4 == 0, named(heavy_load, number // 4), named(ordinary, number - number // 4 - 1))
    mixed = jax.random.permutation(jax.random.fold_in(own, 3), amount)
    donor, receiver = mixed[0:amount // 2 * 2:2], mixed[1:amount // 2 * 2:2]
    margin = jnp.minimum(lengths[donor] - 1, bound - lengths[receiver]) // 2
    margin = jnp.where((donor == sequence[0]) | (receiver == sequence[0]) | (lengths[receiver] == 0), 0, jnp.maximum(margin, 0))
    moved = jax.random.randint(jax.random.fold_in(own, 4), (amount // 2,), 0, 1 << 20) % (margin + 1)
    lengths = lengths.at[donor].add(-moved).at[receiver].add(moved)
    items = jnp.searchsorted(jnp.cumsum(lengths), jnp.arange(rows * top), side="right").astype(jnp.int32)
    listing = items.reshape(top, rows).T
    listing = listing[jax.random.permutation(jax.random.fold_in(own, 1), rows)]
    turn = jax.random.randint(jax.random.fold_in(own, 2), (rows, 1), 0, top)
    return jnp.take_along_axis(listing, (jnp.arange(top)[None, :] + turn) % top, axis=1)


def load_shares(amount, total, most, slope, full):
    loads = [(1 << 20) // math.isqrt(grade ** slope) + 1 for grade in range(1, amount + 1)]
    largest = most if full else min(most, max(-(-total // amount), total * loads[0] // sum(loads)))
    least = 1 if total - largest >= amount - 1 else 0
    holding, surplus = [largest] + [least] * (amount - 1), total - largest - least * (amount - 1)
    while surplus > 0:
        free = [i for i in range(1, amount) if holding[i] < largest] or [i for i in range(1, amount) if holding[i] < most]
        mass, budget = sum([loads[i] for i in free]), surplus
        for i in free:
            more = min(most - holding[i], max(1, budget * loads[i] // mass), surplus)
            holding[i] = holding[i] + more
            surplus = surplus - more
    return np.array(holding)


def gaussian(stream_key, extent, scale, bound, split=(), kind=jnp.bfloat16):
    gain = level_of(stream_key, extent, split, -0.22, 0.18) if split else 1.0
    array = jax.random.normal(stream_key, extent, jnp.float32) * scale * gain
    return jnp.minimum(jnp.maximum(array, -bound), bound).astype(kind)


def setup_inputs(seed: int = 0, part: int = 0) -> dict:
    keys = jax.random.split(jax.random.key(seed), 4)
    part_splits = jax.random.split(jax.random.fold_in(keys[3], part), 4)
    embeddings = gaussian(part_splits[0], (ROWS, D), 1.0, 6.0, ((0, 16),))
    labels_keys = jax.random.split(jax.random.fold_in(part_splits[1], 1), ROWS // ROW_DEV)
    labels_turns = jax.random.permutation(jax.random.fold_in(part_splits[1], 3), ROWS // ROW_DEV)
    labels = jax.vmap(lambda own, number: shared_out(jax.random.fold_in(part_splits[1], 2), own, number, ROW_DEV, CLUSTERS, 1, CAP, 2))(labels_keys, labels_turns).reshape((ROWS, 1))
    priority = with_ends(jax.random.randint(part_splits[2], (ROWS,), 0, 4096), jax.random.fold_in(part_splits[2], 1), 0, 4095).astype(jnp.int32)
    return dict(embeddings=embeddings, labels=labels, priority=priority)


def reference(embeddings, labels, priority):
    row_total = embeddings.shape[0]
    widened = embeddings.astype(jnp.float32)
    unit_rows = (widened * lax.rsqrt(lax.optimization_barrier(jnp.sum(widened * widened, axis=1, keepdims=True)) + 1e-06)).astype(jnp.bfloat16)
    order_key = priority * row_total + jnp.arange(row_total, dtype=jnp.int32)
    row_label = labels[:, 0]
    sorted_index = jnp.argsort(order_key, stable=True).astype(jnp.int32)
    sorted_index = sorted_index[jnp.argsort(row_label[sorted_index], stable=True)].astype(jnp.int32)
    sorted_unit = unit_rows[sorted_index].astype(jnp.float32)
    sorted_label = row_label[sorted_index]
    cluster_start = jnp.searchsorted(sorted_label, sorted_label, side='left').astype(jnp.int32)
    tile_rows = 512
    tile_count = row_total // tile_rows
    positions = jnp.arange(row_total, dtype=jnp.int32)

    def score_tile(query_tile):
        query_start = query_tile * tile_rows
        queries = lax.dynamic_slice_in_dim(sorted_unit, query_start, tile_rows, 0)
        query_label = lax.dynamic_slice_in_dim(sorted_label, query_start, tile_rows, 0)
        query_pos = lax.dynamic_slice_in_dim(positions, query_start, tile_rows, 0)
        first_tile = (cluster_start[query_start] // tile_rows).astype(jnp.int32)

        def absorb_tile(tile_index, running):
            key_start = tile_index * tile_rows
            key_rows = lax.dynamic_slice_in_dim(sorted_unit, key_start, tile_rows, 0)
            key_label = lax.dynamic_slice_in_dim(sorted_label, key_start, tile_rows, 0)
            key_pos = lax.dynamic_slice_in_dim(positions, key_start, tile_rows, 0)
            scores = jnp.dot(queries, key_rows.T, precision=lax.Precision.HIGHEST, preferred_element_type=jnp.float32)
            earlier = (key_label[None, :] == query_label[:, None]) & (key_pos[None, :] < query_pos[:, None])
            return jnp.maximum(running, lax.optimization_barrier(jnp.max(jnp.where(earlier, scores, -1.0), axis=1)))
        return lax.fori_loop(first_tile, query_tile + 1, absorb_tile, jnp.full((tile_rows,), -1.0, jnp.float32))
    best_sorted = lax.map(score_tile, jnp.arange(tile_count, dtype=jnp.int32)).reshape(row_total)
    return jnp.zeros((row_total,), jnp.float32).at[sorted_index].set(best_sorted)
```

```python
import jax
import jax.numpy as jnp
from jax import lax
from jax.experimental import pallas as pl
from jax.experimental.pallas import tpu as pltpu
from jax.sharding import PartitionSpec as P

VMEM_BYTES = 40 * 1024 * 1024


def unit(raw):
    wide = raw.astype(jnp.float32)
    scale = lax.rsqrt(jnp.sum(wide * wide, axis=1, keepdims=True) + 1e-06)
    return (wide * scale).astype(jnp.bfloat16)


def as_column(row):
    parts = [
        jnp.broadcast_to(row[:, i : i + 128], (128, 128)).T for i in range(0, row.shape[1], 128)
    ]
    return jnp.concatenate(parts, axis=0)


def score_block(left, right, left_label, left_key, right_meta):
    scores = lax.dot_general(
        left, right, (((1,), (1,)), ((), ())), preferred_element_type=jnp.float32
    )
    for_left, for_right = None, []
    for i in range(0, scores.shape[1], 128):
        tile = scores[:, i : i + 128]
        label, key = right_meta[0:1, i : i + 128], right_meta[1:2, i : i + 128]
        tile = jnp.where(left_label == label, tile, -1.0)
        earlier = key < left_key
        mine = jnp.where(earlier, tile, -1.0)
        for_left = mine if for_left is None else jnp.maximum(for_left, mine)
        theirs = jnp.where(left_key < key, tile, -1.0)
        for_right.append(jnp.max(theirs, axis=0, keepdims=True))
    return for_left, jnp.concatenate(for_right, axis=1)


def as_row(column_best):
    parts = [
        jnp.max(column_best[i : i + 128, :].T, axis=0, keepdims=True)
        for i in range(0, column_best.shape[0], 128)
    ]
    return jnp.concatenate(parts, axis=1)


def plane_kernel(count, *refs):
    blocks, metas = refs[:count], refs[count : 2 * count]
    unit_out, own_out = refs[2 * count :]
    rows = blocks[0].shape[0]
    own = unit(blocks[0][...])
    own_label, own_key = as_column(metas[0][0:1, :]), as_column(metas[0][1:2, :])
    best = None
    for i in range(count):
        right = own if i == 0 else unit(blocks[i][...])
        unit_out[i * rows : (i + 1) * rows, :] = right
        here, _ = score_block(own, right, own_label, own_key, metas[i][...])
        best = here if best is None else jnp.maximum(best, here)
    own_out[...] = as_row(best)


def pair_kernel(count, reps, has_sum, *refs):
    unit_ref, other_ref, other_meta = refs[:3]
    metas = refs[3 : 3 + count]
    refs = refs[3 + count :]
    sums = refs[:reps] if has_sum else None
    outs = refs[reps:] if has_sum else refs
    other_out = outs[reps]
    rows = other_ref.shape[0]
    other = unit(other_ref[...])
    label, key = as_column(other_meta[0:1, :]), as_column(other_meta[1:2, :])
    best = None
    for i in range(count):
        right = unit_ref[i * rows : (i + 1) * rows, :]
        here, there = score_block(other, right, label, key, metas[i][...])
        best = here if best is None else jnp.maximum(best, here)
        shift, rep = i // reps, i % reps
        if has_sum:
            there = jnp.maximum(there, sums[rep][shift : shift + 1, :])
        outs[rep][shift : shift + 1, :] = there
    other_out[...] = as_row(best)


def kernel_call(kernel, out_shape, operands, flops):
    whole = pl.BlockSpec(memory_space=pltpu.VMEM)
    return pl.pallas_call(
        kernel,
        out_shape=out_shape,
        in_specs=[whole] * len(operands),
        out_specs=[whole] * len(out_shape),
        compiler_params=pltpu.CompilerParams(vmem_limit_bytes=VMEM_BYTES),
        cost_estimate=pl.CostEstimate(
            flops=flops,
            bytes_accessed=sum(o.size * o.dtype.itemsize for o in operands),
            transcendentals=0,
        ),
    )(*operands)


def body(embeddings, labels, priority):
    rows, width = embeddings.shape
    owners, helpers, reps = (lax.axis_size(a) for a in ("cluster", "helper", "rep"))
    row_total = rows * owners * helpers * reps
    count = helpers * reps
    place = lax.axis_index(("cluster", "helper", "rep"))
    order_key = priority * row_total + place * rows + jnp.arange(rows, dtype=jnp.int32)
    meta = jnp.stack([labels[:, 0] + 1, order_key])

    def shifted(value, axis, size, shift):
        return lax.ppermute(value, axis, [((i + shift) % size, i) for i in range(size)])

    steps = [[(i, (i + d) % owners) for i in range(owners)] for d in range(1, (owners + 1) // 2)]
    backs = [[(b, a) for a, b in step] for step in steps]
    if owners % 2 == 0:
        half = owners // 2
        steps.append([(i, i + half) if i % 2 == 0 else (i + half, i) for i in range(half)])
        backs.append([(i, (i + half) % owners) for i in range(owners)])
    others = [lax.ppermute(embeddings, "cluster", step) for step in steps]

    def plane(value):
        result = []
        for h in range(helpers):
            base = value if h == 0 else shifted(value, "helper", helpers, h)
            for r in range(reps):
                result.append(base if r == 0 else shifted(base, "rep", reps, r))
        return result

    blocks = plane(embeddings)
    metas = plane(meta)
    other_metas = [lax.ppermute(meta, "cluster", step) for step in steps]

    f32 = jnp.float32
    units, own_best = kernel_call(
        lambda *refs: plane_kernel(count, *refs),
        [
            jax.ShapeDtypeStruct((count * rows, width), jnp.bfloat16),
            jax.ShapeDtypeStruct((1, rows), f32),
        ],
        blocks + metas,
        2 * count * rows * rows * width,
    )
    sums, returned = [], []
    for other, other_meta, back in zip(others, other_metas, backs):
        has_sum = bool(sums)
        *sums, other_best = kernel_call(
            lambda *refs, has_sum=has_sum: pair_kernel(count, reps, has_sum, *refs),
            [jax.ShapeDtypeStruct((helpers, rows), f32)] * reps
            + [jax.ShapeDtypeStruct((1, rows), f32)],
            [units, other, other_meta] + metas + list(sums),
            2 * count * rows * rows * width,
        )
        returned.append(lax.ppermute(other_best, "cluster", back))
    total = sums[0]
    for r in range(1, reps):
        total = jnp.maximum(total, shifted(sums[r], "rep", reps, reps - r))
    best = jnp.maximum(own_best, total[0:1])
    for h in range(1, helpers):
        best = jnp.maximum(best, shifted(total[h : h + 1], "helper", helpers, helpers - h))
    for value in returned:
        best = jnp.maximum(best, value)
    return best[0]


def solution(mesh):
    axes = ("groups", "cluster", "helper", "rep")
    in_specs = (P(axes, None), P(axes, None), P(axes))
    return jax.shard_map(body, mesh=mesh, in_specs=in_specs, out_specs=P(axes), check_vma=False)
```

```python
import jax
import jax.numpy as jnp
from jax import lax
from jax.experimental import pallas as pl
from jax.experimental.pallas import tpu as pltpu
from jax.sharding import PartitionSpec as P

VMEM_BYTES = 40 * 1024 * 1024
META_ROWS = 8
DIGITS = 4


def prepare_kernel(place, row_total, raw_ref, label_ref, priority_ref, out_ref):
    rows, width = raw_ref.shape
    wide = raw_ref[...].astype(jnp.float32)
    scale = lax.rsqrt(jnp.sum(wide * wide, axis=1, keepdims=True) + 1e-06)
    out_ref[0:rows, :] = (wide * scale).astype(jnp.bfloat16)
    index = lax.broadcasted_iota(jnp.int32, (1, rows), 1)
    key = priority_ref[...] * row_total + place() * rows + index
    digits = jnp.concatenate([(key >> (8 * i)) & 255 for i in range(DIGITS)], axis=1)
    label = jnp.concatenate([label_ref[...] + 1] + [jnp.zeros_like(key)] * (DIGITS - 1), axis=1)
    which = lax.broadcasted_iota(jnp.int32, (META_ROWS, DIGITS * rows), 0)
    extra = jnp.where(which == 0, label, jnp.where(which == 1, digits, 0)).astype(jnp.float32)
    if width > DIGITS * rows:
        zeros = jnp.zeros((META_ROWS, width - DIGITS * rows), jnp.float32)
        extra = jnp.concatenate([extra, zeros], axis=1)
    out_ref[rows : rows + META_ROWS, :] = extra.astype(jnp.bfloat16)


def meta_of(ref, rows):
    extra = ref[rows : rows + META_ROWS, :].astype(jnp.float32).astype(jnp.int32)
    label = extra[0:1, 0:rows]
    key = extra[1:2, 0:rows]
    for i in range(1, DIGITS):
        key = key + (extra[1:2, i * rows : (i + 1) * rows] << (8 * i))
    return label, key


def as_column(row):
    parts = [
        jnp.broadcast_to(row[:, i : i + 128], (128, 128)).T for i in range(0, row.shape[1], 128)
    ]
    return jnp.concatenate(parts, axis=0)


def as_row(column_best):
    parts = [
        jnp.max(column_best[i : i + 128, :].T, axis=0, keepdims=True)
        for i in range(0, column_best.shape[0], 128)
    ]
    return jnp.concatenate(parts, axis=1)


def score_block(left, right, left_label, left_key, label, key):
    scores = lax.dot_general(
        left, right, (((1,), (1,)), ((), ())), preferred_element_type=jnp.float32
    )
    for_left, for_right = None, []
    for i in range(0, scores.shape[1], 128):
        tile = jnp.where(left_label == label[:, i : i + 128], scores[:, i : i + 128], -1.0)
        mine = jnp.where(key[:, i : i + 128] < left_key, tile, -1.0)
        for_left = mine if for_left is None else jnp.maximum(for_left, mine)
        theirs = jnp.where(left_key < key[:, i : i + 128], tile, -1.0)
        for_right.append(jnp.max(theirs, axis=0, keepdims=True))
    return for_left, jnp.concatenate(for_right, axis=1)


def score_kernel(rows, reps, grid, sum_in, left_in, *refs):
    lefts, rights = len(grid), max(max(met) for met in grid if met) + 1
    right_refs, left_refs, refs = refs[:rights], refs[rights : lefts + rights], refs[lefts + rights :]
    old_sums, refs = refs[: reps * sum_in], refs[reps * sum_in :]
    old_lefts, refs = refs[:left_in], refs[left_in:]
    sums, outs = refs[:reps], refs[reps:]
    for r in range(reps):
        sums[r][...] = old_sums[r][...] if sum_in else jnp.full(sums[r].shape, -1.0, jnp.float32)
    for j, met in enumerate(grid):
        left = left_refs[j][0:rows, :]
        left_label, left_key = (as_column(m) for m in meta_of(left_refs[j], rows))
        best = None
        for i in met:
            label, key = meta_of(right_refs[i], rows)
            here, there = score_block(
                left, right_refs[i][0:rows, :], left_label, left_key, label, key
            )
            best = here if best is None else jnp.maximum(best, here)
            if j > 0:
                where = slice(i // reps, i // reps + 1)
                sums[i % reps][where, :] = jnp.maximum(sums[i % reps][where, :], there)
        row = old_lefts[j][...] if j < left_in else None
        if met:
            row = as_row(best) if row is None else jnp.maximum(row, as_row(best))
        outs[j][...] = row


def kernel_call(kernel, out_shape, operands, flops, **options):
    whole = pl.BlockSpec(memory_space=pltpu.VMEM)
    options.setdefault("in_specs", [whole] * len(operands))
    return pl.pallas_call(
        kernel,
        out_shape=out_shape,
        out_specs=[whole] * len(out_shape),
        compiler_params=pltpu.CompilerParams(vmem_limit_bytes=VMEM_BYTES),
        cost_estimate=pl.CostEstimate(
            flops=flops,
            bytes_accessed=sum(o.size * o.dtype.itemsize for o in operands),
            transcendentals=0,
        ),
        **options,
    )(*operands)


def body(embeddings, labels, priority):
    rows, width = embeddings.shape
    owners, helpers, reps = (lax.axis_size(a) for a in ("cluster", "helper", "rep"))
    row_total = rows * owners * helpers * reps
    count = helpers * reps

    def place():
        return lax.axis_index(("cluster", "helper", "rep"))

    (mine,) = kernel_call(
        lambda *refs: prepare_kernel(place, row_total, *refs),
        [jax.ShapeDtypeStruct((rows + META_ROWS, width), jnp.bfloat16)],
        [embeddings, labels.reshape(1, rows), priority.reshape(1, rows)],
        4 * rows * width,
    )

    def shifted(value, axis, size, shift):
        return lax.ppermute(value, axis, [((i + shift) % size, i) for i in range(size)])

    steps = [[(i, (i + d) % owners) for i in range(owners)] for d in range(1, (owners + 1) // 2)]
    backs = [[(b, a) for a, b in step] for step in steps]
    if owners % 2 == 0:
        half = owners // 2
        steps.append([(i, i + half) if i % 2 == 0 else (i + half, i) for i in range(half)])
        backs.append([(i, (i + half) % owners) for i in range(owners)])
    others = [lax.ppermute(mine, "cluster", step) for step in steps]

    def plane_block(h, r):
        pairs = [
            (((i + h) % helpers) * reps + (j + r) % reps, i * reps + j)
            for i in range(helpers)
            for j in range(reps)
        ]
        return lax.ppermute(mine, ("helper", "rep"), pairs) if h or r else mine

    blocks = [plane_block(h, r) for h in range(helpers) for r in range(reps)]

    row = jax.ShapeDtypeStruct((1, rows), jnp.float32)
    per_rep = [jax.ShapeDtypeStruct((helpers, rows), jnp.float32)] * reps

    def score(lefts, grid, sums, bests, flops=None):
        used = max(max(met) for met in grid if met) + 1
        found = kernel_call(
            lambda *refs: score_kernel(rows, reps, grid, bool(sums), len(bests), *refs),
            per_rep + [row] * len(grid),
            [blocks[i] if any(i in met for met in grid) else mine for i in range(used)] + lefts + sums + bests,
            flops or 2 * sum(map(len, grid)) * rows * rows * width,
        )
        return list(found[:reps]), list(found[reps:])

    every = list(range(count))
    far = [i for i in every if i >= reps and i % reps]
    near = [i for i in every if i not in far]
    firsts = [mine] + others[:-1]
    sums, bests = score(firsts, [near] * len(firsts), [], [])
    sums, bests = score([mine] + others, [far] * len(firsts) + [every], sums, bests)
    own_best, *found = bests
    returned = [lax.ppermute(value, "cluster", back) for value, back in zip(found, backs)]
    total = sums[0]
    for r in range(1, reps):
        total = jnp.maximum(total, shifted(sums[r], "rep", reps, reps - r))
    best = jnp.maximum(own_best, total[0:1])
    for h in range(1, helpers):
        best = jnp.maximum(best, shifted(total[h : h + 1], "helper", helpers, helpers - h))
    for value in returned:
        best = jnp.maximum(best, value)
    return best[0]


def solution(mesh):
    axes = ("groups", "cluster", "helper", "rep")
    in_specs = (P(axes, None), P(axes, None), P(axes))
    return jax.shard_map(body, mesh=mesh, in_specs=in_specs, out_specs=P(axes), check_vma=False)
```

```python
import jax
import jax.numpy as jnp
from jax import lax
from jax.experimental import pallas as pl
from jax.experimental.pallas import tpu as pltpu
from jax.sharding import PartitionSpec as P

VMEM_BYTES = 40 * 1024 * 1024
META_ROWS = 8
DIGITS = 4


def prepare_kernel(place, row_total, raw_ref, label_ref, priority_ref, out_ref):
    rows, width = raw_ref.shape
    wide = raw_ref[...].astype(jnp.float32)
    scale = lax.rsqrt(jnp.sum(wide * wide, axis=1, keepdims=True) + 1e-06)
    out_ref[0:rows, :] = (wide * scale).astype(jnp.bfloat16)
    index = lax.broadcasted_iota(jnp.int32, (1, rows), 1)
    key = priority_ref[...] * row_total + place() * rows + index
    digits = jnp.concatenate([(key >> (8 * i)) & 255 for i in range(DIGITS)], axis=1)
    label = jnp.concatenate([label_ref[...] + 1] + [jnp.zeros_like(key)] * (DIGITS - 1), axis=1)
    which = lax.broadcasted_iota(jnp.int32, (META_ROWS, DIGITS * rows), 0)
    extra = jnp.where(which == 0, label, jnp.where(which == 1, digits, 0)).astype(jnp.float32)
    if width > DIGITS * rows:
        zeros = jnp.zeros((META_ROWS, width - DIGITS * rows), jnp.float32)
        extra = jnp.concatenate([extra, zeros], axis=1)
    out_ref[rows : rows + META_ROWS, :] = extra.astype(jnp.bfloat16)


def meta_of(ref, rows):
    extra = ref[rows : rows + META_ROWS, :].astype(jnp.float32).astype(jnp.int32)
    label = extra[0:1, 0:rows]
    key = extra[1:2, 0:rows]
    for i in range(1, DIGITS):
        key = key + (extra[1:2, i * rows : (i + 1) * rows] << (8 * i))
    return label, key


def as_column(row):
    parts = [
        jnp.broadcast_to(row[:, i : i + 128], (128, 128)).T for i in range(0, row.shape[1], 128)
    ]
    return jnp.concatenate(parts, axis=0)


def as_row(column_best):
    parts = [
        jnp.max(column_best[i : i + 128, :].T, axis=0, keepdims=True)
        for i in range(0, column_best.shape[0], 128)
    ]
    return jnp.concatenate(parts, axis=1)


def score_block(left, right, left_label, left_key, label, key):
    scores = lax.dot_general(
        left, right, (((1,), (1,)), ((), ())), preferred_element_type=jnp.float32
    )
    for_left, for_right = None, []
    for i in range(0, scores.shape[1], 128):
        tile = jnp.where(left_label == label[:, i : i + 128], scores[:, i : i + 128], -1.0)
        mine = jnp.where(key[:, i : i + 128] < left_key, tile, -1.0)
        for_left = mine if for_left is None else jnp.maximum(for_left, mine)
        theirs = jnp.where(key[:, i : i + 128] < left_key, -1.0, tile)
        for_right.append(jnp.max(theirs, axis=0, keepdims=True))
    return for_left, jnp.concatenate(for_right, axis=1)


def score_kernel(rows, helpers, reps, grid, sum_in, left_in, sum_out, *refs):
    lefts, rights = len(grid), max(max(met) for met in grid if met) + 1
    left_refs, right_refs, refs = refs[:lefts], refs[lefts : lefts + rights], refs[lefts + rights :]
    old_sums, refs = refs[: reps * sum_in], refs[reps * sum_in :]
    old_lefts, refs = refs[:left_in], refs[left_in:]
    sums, outs = refs[: reps * sum_out], refs[reps * sum_out :]
    for r in range(len(sums)):
        sums[r][...] = old_sums[r][...] if sum_in else jnp.full(sums[r].shape, -1.0, jnp.float32)
    for j, met in enumerate(grid):
        left = left_refs[j][0:rows, :]
        left_label, left_key = (as_column(m) for m in meta_of(left_refs[j], rows))
        best = None
        for i in met:
            label, key = meta_of(right_refs[i], rows)
            here, there = score_block(
                left, right_refs[i][0:rows, :], left_label, left_key, label, key
            )
            best = here if best is None else jnp.maximum(best, here)
            if sum_out:
                rep, where = i // helpers, slice(i % helpers, i % helpers + 1)
                sums[rep][where, :] = jnp.maximum(sums[rep][where, :], there)
        row = old_lefts[j][...] if j < left_in else None
        if met:
            row = as_row(best) if row is None else jnp.maximum(row, as_row(best))
        outs[j][...] = row


def kernel_call(kernel, out_shape, operands, flops, **options):
    whole = pl.BlockSpec(memory_space=pltpu.VMEM)
    options.setdefault("in_specs", [whole] * len(operands))
    return pl.pallas_call(
        kernel,
        out_shape=out_shape,
        out_specs=[whole] * len(out_shape),
        compiler_params=pltpu.CompilerParams(vmem_limit_bytes=VMEM_BYTES),
        cost_estimate=pl.CostEstimate(
            flops=flops,
            bytes_accessed=sum(o.size * o.dtype.itemsize for o in operands),
            transcendentals=0,
        ),
        **options,
    )(*operands)


def body(embeddings, labels, priority):
    rows, width = embeddings.shape
    owners, helpers, reps = (lax.axis_size(a) for a in ("cluster", "helper", "rep"))
    row_total = rows * owners * helpers * reps
    count = helpers * reps

    def place():
        return lax.axis_index(("cluster", "helper", "rep"))

    (mine,) = kernel_call(
        lambda *refs: prepare_kernel(place, row_total, *refs),
        [jax.ShapeDtypeStruct((rows + META_ROWS, width), jnp.bfloat16)],
        [embeddings, labels.reshape(1, rows), priority.reshape(1, rows)],
        4 * rows * width,
    )

    def shifted(value, axis, size, shift):
        return lax.ppermute(value, axis, [((i + shift) % size, i) for i in range(size)])

    steps = [[(i, (i + d) % owners) for i in range(owners)] for d in range(1, (owners + 1) // 2)]
    backs = [[(b, a) for a, b in step] for step in steps]
    if owners % 2 == 0:
        half = owners // 2
        steps.append([(i, i + half) if i % 2 == 0 else (i + half, i) for i in range(half)])
        back = [(b, a) for a, b in steps[-1]]
        idle = sorted({i for i, _ in steps[-1]}), sorted({i for _, i in steps[-1]})
        backs.append(back + list(zip(*idle)))
    others = [lax.ppermute(mine, "cluster", step) for step in steps]

    def plane_block(h, r):
        pairs = [
            (((i + h) % helpers) * reps + (j + r) % reps, i * reps + j)
            for i in range(helpers)
            for j in range(reps)
        ]
        return lax.ppermute(mine, ("helper", "rep"), pairs) if h or r else mine

    blocks = [plane_block(h, r) for r in range(reps) for h in range(helpers)]

    row = jax.ShapeDtypeStruct((1, rows), jnp.float32)
    per_rep = [jax.ShapeDtypeStruct((helpers, rows), jnp.float32)] * reps

    def score(lefts, grid, sums, bests, sum_out=True):
        used = max(max(met) for met in grid if met) + 1
        rights = [blocks[i] if any(i in met for met in grid) else mine for i in range(used)]
        found = kernel_call(
            lambda *refs: score_kernel(rows, helpers, reps, grid, bool(sums), len(bests), sum_out, *refs),
            per_rep * sum_out + [row] * len(grid),
            lefts + rights + sums + bests,
            2 * sum(map(len, grid)) * rows * rows * width,
        )
        return list(found[: reps * sum_out]), list(found[reps * sum_out :])

    every = list(range(count))
    far = [i for i in every if i >= helpers and i % helpers]
    near = [i for i in every if i not in far]
    sums, found = [], []
    if others[1:]:
        sums, found = score(others[:-1], [near] * (len(others) - 1), [], [])
    sums, found = score(others, [far] * (len(others) - 1) + [every], sums, found)
    _, (own_best,) = score([mine], [every], [], [], False)
    returned = [lax.ppermute(v, "cluster", b) for v, b in zip(found[::-1], backs[::-1])]
    total = sums[0]
    for r in range(1, reps):
        total = jnp.maximum(total, shifted(sums[r], "rep", reps, reps - r))
    best = jnp.maximum(own_best, total[0:1])
    for h in range(1, helpers):
        best = jnp.maximum(best, shifted(total[h : h + 1], "helper", helpers, helpers - h))
    for value in returned:
        best = jnp.maximum(best, value)
    return best[0]


def solution(mesh):
    axes = ("groups", "cluster", "helper", "rep")
    in_specs = (P(axes, None), P(axes, None), P(axes))
    return jax.shard_map(body, mesh=mesh, in_specs=in_specs, out_specs=P(axes), check_vma=False)
```

```python
import jax
import jax.numpy as jnp
from jax import lax
from jax.experimental import pallas as pl
from jax.experimental.pallas import tpu as pltpu
from jax.sharding import PartitionSpec as P

VMEM_BYTES = 40 * 1024 * 1024
META_ROWS = 8
DIGITS = 4


def prepare_kernel(place, row_total, raw_ref, label_ref, priority_ref, out_ref):
    rows, width = raw_ref.shape
    wide = raw_ref[...].astype(jnp.float32)
    scale = lax.rsqrt(jnp.sum(wide * wide, axis=1, keepdims=True) + 1e-06)
    out_ref[0:rows, :] = (wide * scale).astype(jnp.bfloat16)
    index = lax.broadcasted_iota(jnp.int32, (1, rows), 1)
    key = priority_ref[...] * row_total + place() * rows + index
    digits = jnp.concatenate([(key >> (8 * i)) & 255 for i in range(DIGITS)], axis=1)
    label = jnp.concatenate([label_ref[...] + 1] + [jnp.zeros_like(key)] * (DIGITS - 1), axis=1)
    which = lax.broadcasted_iota(jnp.int32, (META_ROWS, DIGITS * rows), 0)
    extra = jnp.where(which == 0, label, jnp.where(which == 1, digits, 0)).astype(jnp.float32)
    if width > DIGITS * rows:
        zeros = jnp.zeros((META_ROWS, width - DIGITS * rows), jnp.float32)
        extra = jnp.concatenate([extra, zeros], axis=1)
    out_ref[rows : rows + META_ROWS, :] = extra.astype(jnp.bfloat16)


def meta_of(ref, rows):
    extra = ref[rows : rows + META_ROWS, :].astype(jnp.float32).astype(jnp.int32)
    label = extra[0:1, 0:rows]
    key = extra[1:2, 0:rows]
    for i in range(1, DIGITS):
        key = key + (extra[1:2, i * rows : (i + 1) * rows] << (8 * i))
    return label, key


def as_column(row):
    parts = [
        jnp.broadcast_to(row[:, i : i + 128], (128, 128)).T for i in range(0, row.shape[1], 128)
    ]
    return jnp.concatenate(parts, axis=0)


def as_row(column_best):
    parts = [
        jnp.max(column_best[i : i + 128, :].T, axis=0, keepdims=True)
        for i in range(0, column_best.shape[0], 128)
    ]
    return jnp.concatenate(parts, axis=1)


def score_block(left, right, left_label, left_key, label, key):
    scores = lax.dot_general(
        left, right, (((1,), (1,)), ((), ())), preferred_element_type=jnp.float32
    )
    for_left, for_right = None, []
    for i in range(0, scores.shape[1], 128):
        tile = jnp.where(left_label == label[:, i : i + 128], scores[:, i : i + 128], -1.0)
        mine = jnp.where(key[:, i : i + 128] < left_key, tile, -1.0)
        for_left = mine if for_left is None else jnp.maximum(for_left, mine)
        theirs = jnp.where(key[:, i : i + 128] < left_key, -1.0, tile)
        for_right.append(jnp.max(theirs, axis=0, keepdims=True))
    return for_left, jnp.concatenate(for_right, axis=1)


def score_kernel(rows, helpers, grid, sum_in, left_in, sum_out, *refs):
    lefts, rights = len(grid), max(max(met) for met in grid if met) + 1
    left_refs, right_refs, refs = refs[:lefts], refs[lefts : lefts + rights], refs[lefts + rights :]
    old_sums, refs = refs[: helpers * sum_in], refs[helpers * sum_in :]
    old_lefts, refs = refs[:left_in], refs[left_in:]
    sums, outs = refs[: helpers * sum_out], refs[helpers * sum_out :]
    for h in range(len(sums)):
        sums[h][...] = old_sums[h][...] if sum_in else jnp.full(sums[h].shape, -1.0, jnp.float32)
    for j, met in enumerate(grid):
        left = left_refs[j][0:rows, :]
        left_label, left_key = (as_column(m) for m in meta_of(left_refs[j], rows))
        best = None
        for i in met:
            label, key = meta_of(right_refs[i], rows)
            here, there = score_block(
                left, right_refs[i][0:rows, :], left_label, left_key, label, key
            )
            best = here if best is None else jnp.maximum(best, here)
            if sum_out:
                h, where = i % helpers, slice(i // helpers, i // helpers + 1)
                sums[h][where, :] = jnp.maximum(sums[h][where, :], there)
        row = old_lefts[j][...] if j < left_in else None
        if met:
            row = as_row(best) if row is None else jnp.maximum(row, as_row(best))
        outs[j][...] = row


def kernel_call(kernel, out_shape, operands, flops, **options):
    whole = pl.BlockSpec(memory_space=pltpu.VMEM)
    options.setdefault("in_specs", [whole] * len(operands))
    return pl.pallas_call(
        kernel,
        out_shape=out_shape,
        out_specs=[whole] * len(out_shape),
        compiler_params=pltpu.CompilerParams(vmem_limit_bytes=VMEM_BYTES),
        cost_estimate=pl.CostEstimate(
            flops=flops,
            bytes_accessed=sum(o.size * o.dtype.itemsize for o in operands),
            transcendentals=0,
        ),
        **options,
    )(*operands)


def body(embeddings, labels, priority):
    rows, width = embeddings.shape
    owners, helpers, reps = (lax.axis_size(a) for a in ("cluster", "helper", "rep"))
    row_total = rows * owners * helpers * reps
    count = helpers * reps

    def place():
        return lax.axis_index(("cluster", "helper", "rep"))

    (mine,) = kernel_call(
        lambda *refs: prepare_kernel(place, row_total, *refs),
        [jax.ShapeDtypeStruct((rows + META_ROWS, width), jnp.bfloat16)],
        [embeddings, labels.reshape(1, rows), priority.reshape(1, rows)],
        4 * rows * width,
    )

    def shifted(value, axis, size, shift):
        return lax.ppermute(value, axis, [((i + shift) % size, i) for i in range(size)])

    steps = [[(i, (i + d) % owners) for i in range(owners)] for d in range(1, (owners + 1) // 2)]
    backs = [[(b, a) for a, b in step] for step in steps]
    if owners % 2 == 0:
        half = owners // 2
        steps.append([(i, i + half) if i % 2 == 0 else (i + half, i) for i in range(half)])
        back = [(b, a) for a, b in steps[-1]]
        idle = sorted({i for i, _ in steps[-1]}), sorted({i for _, i in steps[-1]})
        backs.append(back + list(zip(*idle)))
    others = [lax.ppermute(mine, "cluster", step) for step in steps]

    def plane_block(h, r):
        pairs = [
            (((i + h) % helpers) * reps + (j + r) % reps, i * reps + j)
            for i in range(helpers)
            for j in range(reps)
        ]
        return lax.ppermute(mine, ("helper", "rep"), pairs) if h or r else mine

    blocks = [plane_block(h, r) for r in range(reps) for h in range(helpers)]

    row = jax.ShapeDtypeStruct((1, rows), jnp.float32)
    per_helper = [jax.ShapeDtypeStruct((reps, rows), jnp.float32)] * helpers

    def score(lefts, grid, sums, bests, sum_out=True):
        used = max(max(met) for met in grid if met) + 1
        rights = [blocks[i] if any(i in met for met in grid) else mine for i in range(used)]
        found = kernel_call(
            lambda *refs: score_kernel(rows, helpers, grid, bool(sums), len(bests), sum_out, *refs),
            per_helper * sum_out + [row] * len(grid),
            lefts + rights + sums + bests,
            2 * sum(map(len, grid)) * rows * rows * width,
        )
        return list(found[: helpers * sum_out]), list(found[helpers * sum_out :])

    every = list(range(count))
    far = [i for i in every if i >= helpers and i % helpers]
    near = [i for i in every if i not in far]
    sums, found = [], []
    if others[1:]:
        sums, found = score(others[:-1], [near] * (len(others) - 1), [], [])
    sums, found = score(others, [far] * (len(others) - 1) + [every], sums, found)
    _, (own_best,) = score([mine], [every], [], [], False)
    returned = [lax.ppermute(v, "cluster", b) for v, b in zip(found, backs)]
    total = sums[0]
    for h in range(1, helpers):
        total = jnp.maximum(total, shifted(sums[h], "helper", helpers, helpers - h))
    best = jnp.maximum(own_best, total[0:1])
    for r in range(1, reps):
        best = jnp.maximum(best, shifted(total[r : r + 1], "rep", reps, reps - r))
    for value in returned:
        best = jnp.maximum(best, value)
    return best[0]


def solution(mesh):
    axes = ("groups", "cluster", "helper", "rep")
    in_specs = (P(axes, None), P(axes, None), P(axes))
    return jax.shard_map(body, mesh=mesh, in_specs=in_specs, out_specs=P(axes), check_vma=False)
```
